256 devices in a mesh: gx: 8 (over x, core), gy: 4 (over y), gz: 8 (over z).
Axes of the slice: x: 4, y: 4, z: 8, core: 2. Of those that a mesh axis runs over, the one named last changes fastest.
Arguments:
- field: bfloat16 [64, 64, 64, 128], P('gx', 'gy', 'gz'), may hold values from -6 to 6
- coarse_weight: bfloat16 [27, 128, 256], replicated, may hold values from -0.109375 to 0.109375
- fine_weight: bfloat16 [27, 256, 128], replicated, may hold values from -0.078125 to 0.078125
- cotangent: bfloat16 [64, 64, 64, 128], P('gx', 'gy', 'gz'), may hold values from -6 to 6
Outputs:
- output: bfloat16 [64, 64, 64, 128], P('gx', 'gy', 'gz')
- field_grad: bfloat16 [64, 64, 64, 128], P('gx', 'gy', 'gz')
- fine_grad: float32 [27, 256, 128], P(None, None, 'gz')
- coarse_grad: float32 [27, 128, 256], P(None, None, 'gz')
The draws below stay inside these ranges and needn't reach their ends.
All inputs are finite; a program needn't handle non-finite values.
Results may differ from the reference program's by a relative error of at most 0.0051.
Values may be sent and summed in bfloat16 or wider, within the bound.
A program may use at most 128 MiB of HBM per device.

```python
import math
import jax
import jax.numpy as jnp
from jax import lax

CB = 128
CC = 256
NBX = 64
NBY = 64
NBZ = 64


def steps_of(key, dims, pieces, low, top_value):
    gain = 1.0
    for axis_at, blocks in pieces:
        draws = jax.random.uniform(jax.random.fold_in(jax.random.fold_in(key, 6), axis_at), (blocks,), jnp.float32, low / len(pieces), top_value / len(pieces))
        gain = gain * jnp.repeat(jnp.exp(draws), dims[axis_at] // blocks).reshape((-1,) + (1,) * (len(dims) - 1 - axis_at))
    return gain


def scatter_about(own_key, extent, scale, reach, cuts=(), kind=jnp.bfloat16):
    array = scale * jax.random.normal(own_key, extent, jnp.float32)
    if cuts:
        array = array * steps_of(own_key, extent, cuts, -0.22, 0.18)
    return jnp.clip(array, -reach, reach).astype(kind)


def setup_inputs(seed: int = 0) -> dict:
    seeds = jax.random.split(jax.random.key(seed), 5)
    field = scatter_about(seeds[0], (NBX, NBY, NBZ, CB), 1.0, 6.0, ((0, 8), (1, 4), (2, 8)))
    coarse_weight = scatter_about(seeds[1], (27, CB, CC), (27 * CB) ** -0.5, 0.109375)
    fine_weight = scatter_about(seeds[2], (27, CC, CB), (27 * CC) ** -0.5, 0.078125)
    cotangent = scatter_about(seeds[3], (NBX, NBY, NBZ, CB), 1.0, 6.0, ((0, 8), (1, 4), (2, 8)))
    return {"field": field, "coarse_weight": coarse_weight, "fine_weight": fine_weight, "cotangent": cotangent}


def apply_kernel(padded, weight):
    nx, ny, nz = (padded.shape[0] - 2, padded.shape[1] - 2, padded.shape[2] - 2)
    cin = padded.shape[3]
    total = jnp.zeros((nx * ny * nz, weight.shape[2]), jnp.float32)
    for a in range(3):
        for b in range(3):
            for c in range(3):
                piece = padded[a:a + nx, b:b + ny, c:c + nz].reshape(-1, cin)
                total = total + jnp.dot(piece, weight[9 * a + 3 * b + c], preferred_element_type=jnp.float32)
    return total.reshape(nx, ny, nz, weight.shape[2])

def transpose_kernel(padded, weight):
    nx, ny, nz = (padded.shape[0] - 2, padded.shape[1] - 2, padded.shape[2] - 2)
    cin = padded.shape[3]
    total = jnp.zeros((nx * ny * nz, weight.shape[1]), jnp.float32)
    for a in range(3):
        for b in range(3):
            for c in range(3):
                piece = padded[2 - a:2 - a + nx, 2 - b:2 - b + ny, 2 - c:2 - c + nz].reshape(-1, cin)
                total = total + lax.dot_general(piece, weight[9 * a + 3 * b + c], (((1,), (1,)), ((), ())), preferred_element_type=jnp.float32)
    return total.reshape(nx, ny, nz, weight.shape[1])

def kernel_terms(padded, rows):
    nx, ny, nz, cout = rows.shape
    cin = padded.shape[3]
    flat = rows.reshape(-1, cout)
    blocks = []
    for a in range(3):
        for b in range(3):
            for c in range(3):
                piece = padded[a:a + nx, b:b + ny, c:c + nz].reshape(-1, cin)
                blocks.append(lax.dot_general(piece, flat, (((0,), (0,)), ((), ())), preferred_element_type=jnp.float32))
    return jnp.stack(blocks, 0)

def widen(values):
    return jnp.repeat(jnp.repeat(jnp.repeat(values, 2, 0), 2, 1), 2, 2)

def narrow(values):
    nx, ny, nz, chan = values.shape
    return values.reshape(nx // 2, 2, ny // 2, 2, nz // 2, 2, chan).sum(axis=(1, 3, 5))

def border(values):
    return jnp.pad(values, ((1, 1), (1, 1), (1, 1), (0, 0)))

def reference(field, coarse_weight, fine_weight, cotangent):
    pooled = (narrow(field.astype(jnp.float32)) * 0.125).astype(jnp.bfloat16)
    pooled_pad = border(pooled)
    pre = apply_kernel(pooled_pad, coarse_weight)
    hidden = jax.nn.silu(pre).astype(jnp.bfloat16)
    up_pad = border(widen(hidden))
    output = (field.astype(jnp.float32) + apply_kernel(up_pad, fine_weight)).astype(jnp.bfloat16)
    d_up = transpose_kernel(border(cotangent), fine_weight)
    d_hidden = narrow(d_up)
    sig = jax.nn.sigmoid(pre)
    d_pre = (d_hidden * sig * (1.0 + pre * (1.0 - sig))).astype(jnp.bfloat16)
    d_pooled = transpose_kernel(border(d_pre), coarse_weight)
    field_grad = (cotangent.astype(jnp.float32) + widen(d_pooled) * 0.125).astype(jnp.bfloat16)
    cells = field.shape[0] * field.shape[1] * field.shape[2]
    fine_grad = kernel_terms(up_pad, cotangent) / math.sqrt(cells)
    coarse_grad = kernel_terms(pooled_pad, d_pre) / math.sqrt(cells / 8.0)
    return (output, field_grad, fine_grad, coarse_grad)
```

```python
import math

import jax
import jax.numpy as jnp
from jax import lax
from jax.experimental import pallas as pl
from jax.experimental.pallas import tpu as pltpu
from jax.sharding import PartitionSpec as P

MESH = pl.DeviceIdType.MESH
F32 = jnp.float32
BF16 = jnp.bfloat16

EIGHT = [(i, j) for i in (-1, 0, 1) for j in (-1, 0, 1) if (i, j) != (0, 0)]
PAIRS = ((0,), (1, 2), (0, 1), (2,))


def from_side(step, length):
    return pl.ds(1, length) if step == 0 else pl.ds(length if step > 0 else 1, 1)


def to_side(step, length):
    return pl.ds(1, length) if step == 0 else pl.ds(0 if step > 0 else length + 1, 1)


def make_kernel(sizes):
    nx, ny, nz = sizes
    chips = nx // 2
    cells = 1024 * nx * ny * nz

    def kernel(
        field_hbm, w1_hbm, w2_hbm, cot_hbm,
        out_ref, grad_ref, fine_ref, coarse_ref,
        field_v, cot_v, w1, w2, wc,
        cp, zs, zr, tmp, pool_b, pool_s, pool_r, hid_b, hid_s, hid_r, dp_b, dp_s, dp_r,
        im, hb, hi, di, ob, fg,
        g, a1, a2, a3s, a3, r1, b1, b2, b3s, b3, r2, zb, ag,
        in_sem, halo_send, halo_recv, pair_send, pair_recv, rs_send, rs_recv, z_send, z_recv, ag_send, ag_recv,
    ):
        gx, gy, gz = lax.axis_index("gx"), lax.axis_index("gy"), lax.axis_index("gz")
        core = lax.rem(gx, 2)
        chip = gx // 2

        def at(dx, dy, dz):
            return (
                lax.rem(gx + (dx + nx), nx),
                lax.rem(gy + (dy + ny), ny),
                lax.rem(gz + (dz + nz), nz),
            )

        def remote(src, dst, send, recv, device):
            copy = pltpu.make_async_remote_copy(
                src_ref=src, dst_ref=dst, send_sem=send, recv_sem=recv, device_id=device, device_id_type=MESH
            )
            copy.start()
            return copy

        sent = []

        loads = [
            pltpu.make_async_copy(src, dst, in_sem.at[i])
            for i, (src, dst) in enumerate(
                ((field_hbm, field_v), (cot_hbm, cot_v), (w2_hbm, w2), (w1_hbm, w1))
            )
        ]
        for load in loads:
            load.start()

        partners = {(i, j, 0) for i, j in EIGHT} | {(i, 0, j) for i, j in EIGHT} | {(0, 0, 1), (0, 0, nz - 1)}
        partners = {(i % nx, j % ny, k % nz) for i, j, k in partners}
        partners |= {(0, 0, k) for k in range(1, nz)}
        partners |= {(2 * i, j, 0) for i in range(chips) for j in range(ny) if (i, j) != (0, 0)}
        barrier = pltpu.get_barrier_semaphore()
        for step in sorted(partners):
            pl.semaphore_signal(barrier, inc=1, device_id=at(*step), device_id_type=MESH)

        loads[0].wait()
        for x in range(4):
            pair = field_v[2 * x].astype(F32) + field_v[2 * x + 1].astype(F32)
            pair = pair.reshape(8, 2, 8, 128)
            tmp[x] = (pair[:, 0] + pair[:, 1]).reshape(64, 128)
        for z in range(4):
            total = tmp[:, pl.ds(2 * z, 8, stride=8), :] + tmp[:, pl.ds(2 * z + 1, 8, stride=8), :]
            pool_b[0, 1:5, 1 + z, 8:16, :] = (total * 0.125).astype(BF16).astype(F32)
        loads[1].wait()
        for x in range(8):
            cp[1 + x, 8:136, :] = cot_v[x].astype(F32)

        pl.semaphore_wait(barrier, len(partners))

        def start_xz(buf, e):
            copies = []
            for i, (dx, dz) in enumerate(EIGHT):
                copies.append(
                    remote(
                        buf.at[:, from_side(dx, 4), from_side(dz, 4), pl.ds(8, 8), :],
                        buf.at[:, to_side(dx, 4), to_side(dz, 4), pl.ds(8, 8), :],
                        halo_send.at[e, i], halo_recv.at[e, i], at(dx, 0, dz),
                    )
                )
            sent.extend(copies)
            return copies

        def start_y(buf, s, r, e, copies):
            for copy in copies:
                copy.wait_recv()

            @pl.when(gx == 0)
            def _():
                buf[:, 0, :, 8:16, :] = jnp.zeros_like(buf[:, 0, :, 8:16, :])

            @pl.when(gx == nx - 1)
            def _():
                buf[:, 5, :, 8:16, :] = jnp.zeros_like(buf[:, 5, :, 8:16, :])

            @pl.when(gz == 0)
            def _():
                buf[:, :, 0, 8:16, :] = jnp.zeros_like(buf[:, :, 0, 8:16, :])

            @pl.when(gz == nz - 1)
            def _():
                buf[:, :, 5, 8:16, :] = jnp.zeros_like(buf[:, :, 5, 8:16, :])

            flat = buf.reshape(buf.shape[0], 864, 128)
            for h in range(buf.shape[0]):
                s[0, h, 0:36, :] = flat[h, pl.ds(8, 36, stride=24), :]
                s[1, h, 0:36, :] = flat[h, pl.ds(15, 36, stride=24), :]
            below = remote(s.at[0], r.at[1], halo_send.at[e, 8], halo_recv.at[e, 8], at(0, -1, 0))
            above = remote(s.at[1], r.at[0], halo_send.at[e, 9], halo_recv.at[e, 9], at(0, 1, 0))
            sent.extend((below, above))
            return (above, below)

        def finish_y(buf, r, copies):
            for copy in copies:
                copy.wait_recv()

            @pl.when(gy == 0)
            def _():
                r[0] = jnp.zeros_like(r[0])

            @pl.when(gy == ny - 1)
            def _():
                r[1] = jnp.zeros_like(r[1])

            flat = buf.reshape(buf.shape[0], 864, 128)
            for h in range(buf.shape[0]):
                flat[h, pl.ds(7, 36, stride=24), :] = r[0, h, 0:36, :]
                flat[h, pl.ds(16, 36, stride=24), :] = r[1, h, 0:36, :]

        def tap(buf, h, a, b, c):
            return buf[h, a : a + 4, c : c + 4, 7 + b : 15 + b, :].reshape(128, 128).astype(BF16)

        pool_xz = start_xz(pool_b, 0)
        cot_xy = []
        for i, (dx, dy) in enumerate(EIGHT):
            sy = pl.ds(8, 128) if dy == 0 else pl.ds(128 if dy > 0 else 8, 8)
            ty = pl.ds(8, 128) if dy == 0 else pl.ds(0 if dy > 0 else 136, 8)
            cot_xy.append(
                remote(
                    cp.at[from_side(dx, 8), sy, :], cp.at[to_side(dx, 8), ty, :],
                    halo_send.at[3, i], halo_recv.at[3, i], at(dx, dy, 0),
                )
            )
        sent.extend(cot_xy)

        pool_y = start_y(pool_b, pool_s, pool_r, 0, pool_xz)

        for copy in cot_xy:
            copy.wait_recv()

        @pl.when(gx == 0)
        def _():
            cp[0] = jnp.zeros_like(cp[0])

        @pl.when(gx == nx - 1)
        def _():
            cp[9] = jnp.zeros_like(cp[9])

        @pl.when(gy == 0)
        def _():
            cp[:, 0:8, :] = jnp.zeros_like(cp[:, 0:8, :])

        @pl.when(gy == ny - 1)
        def _():
            cp[:, 136:144, :] = jnp.zeros_like(cp[:, 136:144, :])

        cp[:, 144:192, :] = jnp.zeros_like(cp[:, 144:192, :])
        zs[0] = cp[:, pl.ds(0, 24, stride=8), :]
        zs[1] = cp[:, pl.ds(7, 24, stride=8), :]
        z_below = remote(zs.at[0], zr.at[1], halo_send.at[3, 8], halo_recv.at[3, 8], at(0, 0, -1))
        z_above = remote(zs.at[1], zr.at[0], halo_send.at[3, 9], halo_recv.at[3, 9], at(0, 0, 1))
        sent.extend((z_below, z_above))

        loads[2].wait()

        def combine(i, carry):
            rows = pl.ds(pl.multiple_of(i * 16, 16), 16)
            low = pl.ds(pl.multiple_of(i * 16, 16), 16)
            high = pl.ds(pl.multiple_of(256 + i * 16, 16), 16)

            def spread(parts):
                return (parts[0], parts[1] + parts[2], parts[0] + parts[1], parts[2])

            by_ab = [[spread([w2[9 * a + 3 * b + c, rows, :].astype(F32) for c in range(3)]) for b in range(3)] for a in range(3)]
            by_a = [[spread([by_ab[a][b][c] for b in range(3)]) for c in range(4)] for a in range(3)]
            for b in range(4):
                for c in range(4):
                    for a, value in enumerate(spread([by_a[a][c][b] for a in range(3)])):
                        parity = (a // 2) * 4 + (b // 2) * 2 + c // 2
                        wc[parity, (a % 2) * 2 + b % 2, high if c % 2 else low, :] = value.astype(BF16)
            return carry

        lax.fori_loop(0, 16, combine, 0)

        finish_y(pool_b, pool_r, pool_y)
        for k in range(27):
            im[0, 0:128, k * 128 : (k + 1) * 128] = tap(pool_b, 0, k // 9, k // 3 % 3, k % 3)
        loads[3].wait()
        pre = jnp.dot(im[0, 0:128, :], w1[...].reshape(3456, 256), preferred_element_type=F32)
        sig = 1.0 / (1.0 + jnp.exp(-pre))
        hidden = (pre * sig).astype(BF16)
        slope = sig * (1.0 + pre * (1.0 - sig))
        hb[1, 0:128, :] = hidden
        wide = hidden.astype(F32).reshape(4, 4, 8, 256)
        hid_b[0, 1:5, 1:5, 8:16, :] = wide[..., 0:128]
        hid_b[1, 1:5, 1:5, 8:16, :] = wide[..., 128:256]
        hid_xz = start_xz(hid_b, 1)

        z_below.wait_recv()
        z_above.wait_recv()

        @pl.when(gz == 0)
        def _():
            zr[0] = jnp.zeros_like(zr[0])

        @pl.when(gz == nz - 1)
        def _():
            zr[1] = jnp.zeros_like(zr[1])

        def windows(x, carry):
            rows = pl.ds(pl.multiple_of(x * 32, 32), 32)
            for a in range(3):
                planes = pl.ds(2 * x + 2 - a, 2)
                sums = []
                for z in range(10):
                    columns = []
                    for y in range(4):
                        if z == 0:
                            value = zr[0, planes, pl.ds(y, 8, stride=2), :]
                        elif z == 9:
                            value = zr[1, planes, pl.ds(y, 8, stride=2), :]
                        else:
                            value = cp[planes, pl.ds(y * 8 + z - 1, 8, stride=16), :]
                        columns.append(value[0] + value[1])
                    sums.append([columns[2 - b] + columns[3 - b] for b in range(3)])
                for b in range(3):
                    for c in range(3):
                        k = 9 * a + 3 * b + c
                        value = jnp.concatenate(
                            [sums[2 * z + 2 - c][b] + sums[2 * z + 3 - c][b] for z in range(4)], axis=0
                        )
                        im[1, rows, k * 128 : (k + 1) * 128] = value.astype(BF16)
            return carry

        lax.fori_loop(0, 4, windows, 0)

        other = (gx + 1 - 2 * core, gy, gz)
        pair_im = remote(
            im.at[core, pl.ds(0, 128), :], im.at[core, pl.ds(128, 128), :], pair_send.at[0], pair_recv.at[0], other
        )

        d_hidden = jnp.zeros((128, 256), F32)
        for k in range(27):
            d_hidden = d_hidden + lax.dot_general(
                im[1, 0:128, k * 128 : (k + 1) * 128], w2[k], (((1,), (1,)), ((), ())), preferred_element_type=F32
            )
        d_pre = (d_hidden * slope).astype(BF16)
        hb[0, 0:128, :] = d_pre
        pair_hb = remote(
            hb.at[core, pl.ds(0, 128), :], hb.at[core, pl.ds(128, 128), :], pair_send.at[1], pair_recv.at[1], other
        )
        wide = d_pre.astype(F32).reshape(4, 4, 8, 256)
        dp_b[0, 1:5, 1:5, 8:16, :] = wide[..., 0:128]
        dp_b[1, 1:5, 1:5, 8:16, :] = wide[..., 128:256]
        dp_xz = start_xz(dp_b, 2)
        hid_y = start_y(hid_b, hid_s, hid_r, 1, hid_xz)

        pair_im.wait_recv()
        pair_hb.wait_recv()
        g[:, :, 27] = jnp.zeros((2, 8, 16, 128), BF16)

        @pl.when(core == 0)
        def _():
            right = hb[1]
            for k in range(27):
                value = lax.dot_general(
                    im[1, :, k * 128 : (k + 1) * 128], right, (((0,), (0,)), ((), ())), preferred_element_type=F32
                ).astype(BF16)
                value = value.reshape(8, 16, 256)
                g[0, :, k] = value[..., 0:128]
                g[1, :, k] = value[..., 128:256]

        @pl.when(core == 1)
        def _():
            left = hb[0].astype(F32).T.astype(BF16)
            for k in range(27):
                value = jnp.dot(left, im[0, :, k * 128 : (k + 1) * 128], preferred_element_type=F32).astype(BF16)
                value = value.reshape(8, 2, 16, 128)
                g[0, :, k] = value[:, 0]
                g[1, :, k] = value[:, 1]

        def ring(axis, step):
            return at(2 * step, 0, 0) if axis == 0 else at(0, step, 0)

        def place(axis, step):
            return lax.rem(chip + step + 4, 4) if axis == 0 else lax.rem(gy + step + 4, 4)

        def rs_first(src, first, second, units, stage):
            waiting = {}
            for h in range(2):
                axis = (h + stage) % 2
                for i, d in enumerate((1, -1)):
                    waiting[h, i] = (
                        remote(
                            src.at[h, pl.ds(4 * i, 4), pl.ds(units * place(axis, 2), units)], first.at[h, i],
                            rs_send.at[stage, h, i, 0], rs_recv.at[stage, h, i, 0], ring(axis, d),
                        ),
                        remote(
                            src.at[h, pl.ds(4 - 4 * i, 4), pl.ds(units * place(axis, d), units)], second.at[h, i],
                            rs_send.at[stage, h, i, 1], rs_recv.at[stage, h, i, 1], ring(axis, d),
                        ),
                    )
                    sent.extend(waiting[h, i])
            return waiting

        def rs_relay(src, first, out, third, units, stage, waiting):
            relays = {}
            for h in range(2):
                axis = (h + stage) % 2
                for i, d in enumerate((1, -1)):
                    waiting[h, i][0].wait_recv()
                    mine = src[h, 4 * i : 4 * i + 4, pl.ds(units * place(axis, d), units)]
                    out[h, i] = (mine.astype(F32) + first[h, i].astype(F32)).astype(BF16)
                    relays[h, i] = remote(
                        out.at[h, i], third.at[h, i],
                        rs_send.at[stage, h, i, 2], rs_recv.at[stage, h, i, 2], ring(axis, d),
                    )
                    sent.append(relays[h, i])
            return relays

        def rs_last(src, second, third, units, stage, waiting, relays, h, i):
            axis = (h + stage) % 2
            waiting[h, 1 - i][1].wait_recv()
            relays[h, i].wait_recv()
            mine = src[h, 4 * i : 4 * i + 4, pl.ds(units * place(axis, 0), units)]
            total = mine.astype(F32) + second[h, 1 - i].astype(F32) + third[h, i].astype(F32)
            return total.astype(BF16)

        first = rs_first(g, a1, a2, 7, 0)

        dp_y = start_y(dp_b, dp_s, dp_r, 2, dp_xz)
        finish_y(hid_b, hid_r, hid_y)
        for k in range(27):
            for h in range(2):
                hi[:, k * 256 + h * 128 : k * 256 + (h + 1) * 128] = tap(hid_b, h, k // 9, k // 3 % 3, k % 3)

        relays = rs_relay(g, a1, a3s, a3, 7, 0, first)

        for parity in range(8):
            pa, pb, pc = parity // 4, parity // 2 % 2, parity % 2
            total = jnp.zeros((128, 128), F32)
            for side in range(4):
                k = 9 * (pa + side // 2) + 3 * (pb + side % 2) + pc
                total = total + jnp.dot(hi[:, k * 256 : k * 256 + 512], wc[parity, side], preferred_element_type=F32)
            total = total.reshape(4, 4, 8, 128)
            for z in range(4):
                ob[:, pa, pl.ds(pb * 8 + 2 * z + pc, 8, stride=16), :] = total[:, z]
        for x in range(8):
            out_ref[x] = (field_v[x].astype(F32) + ob[x // 2, x % 2]).astype(BF16)

        r1[:, :, 7] = jnp.zeros((2, 8, 16, 128), BF16)
        for h in range(2):
            for i in range(2):
                r1[h, 4 * i : 4 * i + 4, 0:7] = rs_last(g, a2, a3, 7, 0, first, relays, h, i)
        first = rs_first(r1, b1, b2, 2, 1)

        finish_y(dp_b, dp_r, dp_y)
        for k in range(27):
            for h in range(2):
                di[:, k * 256 + h * 128 : k * 256 + (h + 1) * 128] = tap(dp_b, h, k // 9, k // 3 % 3, k % 3)

        relays = rs_relay(r1, b1, b3s, b3, 2, 1, first)

        total = jnp.zeros((128, 128), F32)
        for k in range(27):
            total = total + lax.dot_general(
                di[:, k * 256 : (k + 1) * 256], w1[26 - k], (((1,), (1,)), ((), ())), preferred_element_type=F32
            )
        total = (total * 0.125).reshape(4, 4, 8, 128)
        for z in range(4):
            for j in range(4):
                fg[:, pl.ds(j // 2 * 8 + 2 * z + j % 2, 8, stride=16), :] = total[:, z]
        for x in range(8):
            grad_ref[x] = (cot_v[x].astype(F32) + fg[x // 2]).astype(BF16)

        for h in range(2):
            for i in range(2):
                r2[4 * i : 4 * i + 4, h] = rs_last(r1, b2, b3, 2, 1, first, relays, h, i)

        ups = []
        for d in range(1, nz):
            ups.append(
                remote(
                    r2.at[lax.rem(gz + d, nz)], zb.at[gz], z_send.at[d - 1], z_recv.at[d - 1], at(0, 0, d)
                )
            )
        sent.extend(ups)
        zb[gz] = r2[gz]
        for copy in ups:
            copy.wait_recv()
        total = zb[0].astype(F32)
        for j in range(1, nz):
            total = total + zb[j].astype(F32)
        scale = jnp.where(core == 0, F32(1.0 / math.sqrt(cells)), F32(1.0 / math.sqrt(cells / 8.0)))
        mine = chip * ny + gy
        ag[core, mine] = total * scale

        gathers = []
        for dx in range(chips):
            for dy in range(ny):
                if (dx, dy) != (0, 0):
                    n = dx * ny + dy - 1
                    gathers.append(
                        remote(
                            ag.at[core, mine], ag.at[core, mine], ag_send.at[n], ag_recv.at[n], at(2 * dx, dy, 0)
                        )
                    )
        sent.extend(gathers)
        for copy in gathers:
            copy.wait_recv()
        last = remote(ag.at[core], ag.at[core], pair_send.at[2], pair_recv.at[2], other)
        sent.extend((pair_im, pair_hb, last))
        last.wait_recv()
        for k in range(27):
            j = k % 7
            for h in range(2):
                src = k // 7 * 4 + j // 2 if h == 0 else j // 2 * 4 + k // 7
                fine_ref[k, :, h * 128 : (h + 1) * 128] = ag[0, src, h, j % 2]
                coarse_ref[k, 16 * h : 16 * h + 16, :] = ag[1, src, h, j % 2]
        for copy in sent:
            copy.wait_send()

    return kernel


def solution(mesh):
    sizes = (mesh.shape["gx"], mesh.shape["gy"], mesh.shape["gz"])
    dma = pltpu.SemaphoreType.DMA

    def local(field, coarse_weight, fine_weight, cotangent):
        v = pltpu.VMEM
        scratch = [
            v((8, 128, 128), BF16), v((8, 128, 128), BF16), v((27, 128, 256), BF16), v((27, 256, 128), BF16),
            v((8, 4, 512, 128), BF16),
            v((10, 192, 128), F32), v((2, 10, 24, 128), F32), v((2, 10, 24, 128), F32), v((4, 64, 128), F32),
            v((1, 6, 6, 24, 128), F32), v((2, 1, 40, 128), F32), v((2, 1, 40, 128), F32),
            v((2, 6, 6, 24, 128), F32), v((2, 2, 40, 128), F32), v((2, 2, 40, 128), F32),
            v((2, 6, 6, 24, 128), F32), v((2, 2, 40, 128), F32), v((2, 2, 40, 128), F32),
            v((2, 256, 3456), BF16), v((2, 256, 256), BF16), v((128, 6912), BF16), v((128, 6912), BF16),
            v((4, 2, 128, 128), F32), v((4, 128, 128), F32),
            v((2, 8, 28, 16, 128), BF16),
            v((2, 2, 4, 7, 16, 128), BF16), v((2, 2, 4, 7, 16, 128), BF16),
            v((2, 2, 4, 7, 16, 128), BF16), v((2, 2, 4, 7, 16, 128), BF16),
            v((2, 8, 8, 16, 128), BF16),
            v((2, 2, 4, 2, 16, 128), BF16), v((2, 2, 4, 2, 16, 128), BF16),
            v((2, 2, 4, 2, 16, 128), BF16), v((2, 2, 4, 2, 16, 128), BF16),
            v((8, 2, 2, 16, 128), BF16), v((8, 2, 2, 16, 128), BF16), v((2, 16, 2, 2, 16, 128), F32),
            dma((4,)), dma((4, 10)), dma((4, 10)), dma((3,)), dma((3,)),
            dma((2, 2, 2, 3)), dma((2, 2, 2, 3)), dma((7,)), dma((7,)), dma((15,)), dma((15,)),
        ]
        anywhere = pl.BlockSpec(memory_space=pl.ANY)
        inside = pl.BlockSpec(memory_space=pltpu.VMEM)
        output, field_grad, fine, coarse = pl.pallas_call(
            make_kernel(sizes),
            out_shape=(
                jax.ShapeDtypeStruct((8, 128, 128), BF16),
                jax.ShapeDtypeStruct((8, 128, 128), BF16),
                jax.ShapeDtypeStruct((27, 16, 256), F32),
                jax.ShapeDtypeStruct((27, 32, 128), F32),
            ),
            in_specs=[anywhere] * 4,
            out_specs=(inside,) * 4,
            scratch_shapes=scratch,
            compiler_params=pltpu.CompilerParams(
                collective_id=0, has_side_effects=True, vmem_limit_bytes=56 * 1024 * 1024
            ),
        )(field.reshape(8, 128, 128), coarse_weight, fine_weight, cotangent.reshape(8, 128, 128))
        return (
            output.reshape(8, 16, 8, 128),
            field_grad.reshape(8, 16, 8, 128),
            fine.transpose(0, 2, 1),
            coarse.transpose(0, 2, 1),
        )

    placed = (P("gx", "gy", "gz", None), P(), P(), P("gx", "gy", "gz", None))
    return jax.shard_map(
        local,
        mesh=mesh,
        in_specs=placed,
        out_specs=(
            P("gx", "gy", "gz", None),
            P("gx", "gy", "gz", None),
            P(None, None, "gz"),
            P(None, None, "gz"),
        ),
        check_vma=False,
    )
```

```python
import math

import jax
import jax.numpy as jnp
from jax import lax
from jax.experimental import pallas as pl
from jax.experimental.pallas import tpu as pltpu
from jax.sharding import PartitionSpec as P

MESH = pl.DeviceIdType.MESH
F32 = jnp.float32
BF16 = jnp.bfloat16

SIDES = (-1, 0, 1)
EIGHT = [(i, j) for i in SIDES for j in SIDES if (i, j) != (0, 0)]
NEAR = sorted(((i, j, k) for i in SIDES for j in SIDES for k in SIDES if (i, j, k) != (0, 0, 0)), key=lambda p: -sum(map(abs, p)))
PAIRS = ((0,), (1, 2), (0, 1), (2,))


def from_side(step, length):
    return pl.ds(1, length) if step == 0 else pl.ds(length if step > 0 else 1, 1)


def to_side(step, length):
    return pl.ds(1, length) if step == 0 else pl.ds(0 if step > 0 else length + 1, 1)


def make_kernel(sizes):
    nx, ny, nz = sizes
    chips = nx // 2
    cells = 1024 * nx * ny * nz

    def kernel(
        field_hbm, w1_hbm, w2_hbm, cot_hbm,
        out_hbm, grad_hbm, ag,
        field_v, cot_v, w1, w2, wc, out_v, grad_v,
        cp, zs, zq, tmp, pool_b, hid_b, hid_s, hid_r, dp_b, dp_s, dp_r,
        im, hb, hi, di, ob, fg,
        g, a1, a2, a3s, a3, r1, gb, r2, zb,
        in_sem, out_sem, halo_send, halo_recv, pair_send, pair_recv, fwd_send, fwd_recv, rs_send, rs_recv, z_send, z_recv, ag_send, ag_recv,
    ):
        gx, gy, gz = lax.axis_index("gx"), lax.axis_index("gy"), lax.axis_index("gz")
        core = lax.rem(gx, 2)
        chip = gx // 2

        def at(dx, dy, dz):
            return (
                lax.rem(gx + (dx + nx), nx),
                lax.rem(gy + (dy + ny), ny),
                lax.rem(gz + (dz + nz), nz),
            )

        def plan(src, dst, send, recv, device):
            return pltpu.make_async_remote_copy(
                src_ref=src, dst_ref=dst, send_sem=send, recv_sem=recv, device_id=device, device_id_type=MESH
            )

        def remote(*where):
            copy = plan(*where)
            copy.start()
            return copy

        other = (gx + 1 - 2 * core, gy, gz)
        sent = []

        def drain():
            for copy in sent:
                copy.wait_send()
            sent.clear()

        def hops(p):
            return min(p[0], chips - p[0]) + min(p[1], ny - p[1])

        loads = [
            pltpu.make_async_copy(src, dst, in_sem.at[i])
            for i, (src, dst) in enumerate(
                ((field_hbm, field_v), (cot_hbm, cot_v), (w2_hbm, w2), (w1_hbm, w1))
            )
        ]
        for load in loads:
            load.start()

        partners = {(i % nx, j % ny, k % nz) for i, j, k in NEAR}
        partners |= {(0, 0, k) for k in range(1, nz)}
        partners |= {(2 * i, j, 0) for i in range(chips) for j in range(ny) if (i, j) != (0, 0)}
        crossing = sorted(((i, j) for i in range(chips) for j in range(ny) if hops((i, j)) > 2))
        barrier = pltpu.get_barrier_semaphore()
        for step in sorted(partners):
            pl.semaphore_signal(barrier, inc=1, device_id=at(*step), device_id_type=MESH)
        for i, j in crossing:
            x, y, z = at(2 * i, j, 0)
            pl.semaphore_signal(barrier, inc=1, device_id=(x + 1 - 2 * core, y, z), device_id_type=MESH)

        loads[0].wait()
        for x in range(4):
            pair = field_v[2 * x].astype(F32) + field_v[2 * x + 1].astype(F32)
            pair = pair.reshape(8, 2, 8, 128)
            tmp[x] = (pair[:, 0] + pair[:, 1]).reshape(64, 128)
        for z in range(4):
            total = tmp[:, pl.ds(2 * z, 8, stride=8), :] + tmp[:, pl.ds(2 * z + 1, 8, stride=8), :]
            pool_b[0, 1:5, 1 + z, 8:16, :] = (total * 0.125).astype(BF16).astype(F32)
        loads[1].wait()
        for x in range(8):
            cp[1 + x, 8:136, :] = cot_v[x].astype(F32)
        zs[0] = cp[1:9, pl.ds(8, 16, stride=8), :]
        zs[1] = cp[1:9, pl.ds(15, 16, stride=8), :]

        pl.semaphore_wait(barrier, len(partners) + len(crossing))

        def start_xz(buf, e):
            copies = []
            for i, (dx, dz) in enumerate(EIGHT):
                copies.append(
                    remote(
                        buf.at[:, from_side(dx, 4), from_side(dz, 4), pl.ds(8, 8), :],
                        buf.at[:, to_side(dx, 4), to_side(dz, 4), pl.ds(8, 8), :],
                        halo_send.at[e, i], halo_recv.at[e, i], at(dx, 0, dz),
                    )
                )
            sent.extend(copies)
            return copies

        def start_y(buf, s, r, e, copies):
            for copy in copies:
                copy.wait_recv()

            @pl.when(gx == 0)
            def _():
                buf[:, 0, :, 8:16, :] = jnp.zeros_like(buf[:, 0, :, 8:16, :])

            @pl.when(gx == nx - 1)
            def _():
                buf[:, 5, :, 8:16, :] = jnp.zeros_like(buf[:, 5, :, 8:16, :])

            @pl.when(gz == 0)
            def _():
                buf[:, :, 0, 8:16, :] = jnp.zeros_like(buf[:, :, 0, 8:16, :])

            @pl.when(gz == nz - 1)
            def _():
                buf[:, :, 5, 8:16, :] = jnp.zeros_like(buf[:, :, 5, 8:16, :])

            flat = buf.reshape(buf.shape[0], 864, 128)
            for h in range(buf.shape[0]):
                s[0, h, 0:36, :] = flat[h, pl.ds(8, 36, stride=24), :]
                s[1, h, 0:36, :] = flat[h, pl.ds(15, 36, stride=24), :]
            below = remote(s.at[0], r.at[1], halo_send.at[e, 8], halo_recv.at[e, 8], at(0, -1, 0))
            above = remote(s.at[1], r.at[0], halo_send.at[e, 9], halo_recv.at[e, 9], at(0, 1, 0))
            sent.extend((below, above))
            return (above, below)

        def finish_y(buf, r, copies):
            for copy in copies:
                copy.wait_recv()

            @pl.when(gy == 0)
            def _():
                r[0] = jnp.zeros_like(r[0])

            @pl.when(gy == ny - 1)
            def _():
                r[1] = jnp.zeros_like(r[1])

            flat = buf.reshape(buf.shape[0], 864, 128)
            for h in range(buf.shape[0]):
                flat[h, pl.ds(7, 36, stride=24), :] = r[0, h, 0:36, :]
                flat[h, pl.ds(16, 36, stride=24), :] = r[1, h, 0:36, :]

        def tap(buf, h, a, b, c):
            return buf[h, a : a + 4, c : c + 4, 7 + b : 15 + b, :].reshape(128, 128).astype(BF16)

        def send_pool(i):
            dx, dy, dz = NEAR[i]
            return remote(
                pool_b.at[:, from_side(dx, 4), from_side(dz, 4), pl.ds(8, 8), :],
                pool_b.at[:, to_side(dx, 4), to_side(dz, 4), pl.ds(8 - 8 * dy, 8), :],
                halo_send.at[0, i], halo_recv.at[0, i], at(dx, dy, dz),
            )

        def send_cot(i):
            dx, dy, dz = NEAR[i]
            if dz == 0:
                sy = pl.ds(8, 128) if dy == 0 else pl.ds(128 if dy > 0 else 8, 8)
                ty = pl.ds(8, 128) if dy == 0 else pl.ds(0 if dy > 0 else 136, 8)
                src, dst = cp.at[from_side(dx, 8), sy, :], cp.at[to_side(dx, 8), ty, :]
            else:
                sx = pl.ds(0, 8) if dx == 0 else pl.ds(7 if dx > 0 else 0, 1)
                sy = pl.ds(0, 16) if dy == 0 else pl.ds(8 if dy > 0 else 0, 8)
                ty = pl.ds(8, 16) if dy == 0 else pl.ds(0 if dy > 0 else 24, 8)
                src = zs.at[1 if dz > 0 else 0, sx, sy, :]
                dst = zq.at[0 if dz > 0 else 1, to_side(dx, 8), ty, :]
            return remote(src, dst, halo_send.at[3, i], halo_recv.at[3, i], at(dx, dy, dz))

        wide = [i for i, (dx, dy, dz) in enumerate(NEAR) if (dx, dy) == (0, 0)]
        cots = [send_cot(i) for i in wide]
        pools = [send_pool(i) for i in range(26)]
        cots += [send_cot(i) for i in range(26) if i not in wide]
        sent.extend(pools + cots)

        loads[2].wait()

        def combine(i, carry):
            rows = pl.ds(pl.multiple_of(i * 16, 16), 16)
            low = pl.ds(pl.multiple_of(i * 16, 16), 16)
            high = pl.ds(pl.multiple_of(256 + i * 16, 16), 16)

            def spread(parts):
                return (parts[0], parts[1] + parts[2], parts[0] + parts[1], parts[2])

            by_ab = [[spread([w2[9 * a + 3 * b + c, rows, :].astype(F32) for c in range(3)]) for b in range(3)] for a in range(3)]
            by_a = [[spread([by_ab[a][b][c] for b in range(3)]) for c in range(4)] for a in range(3)]
            for b in range(4):
                for c in range(4):
                    for a, value in enumerate(spread([by_a[a][c][b] for a in range(3)])):
                        parity = (a // 2) * 4 + (b // 2) * 2 + c // 2
                        wc[parity, (a % 2) * 2 + b % 2, high if c % 2 else low, :] = value.astype(BF16)
            return carry

        lax.fori_loop(0, 16, combine, 0)

        for copy in pools:
            copy.wait_recv()

        @pl.when(gx == 0)
        def _():
            pool_b[:, 0] = jnp.zeros_like(pool_b[:, 0])

        @pl.when(gx == nx - 1)
        def _():
            pool_b[:, 5] = jnp.zeros_like(pool_b[:, 5])

        @pl.when(gz == 0)
        def _():
            pool_b[:, :, 0] = jnp.zeros_like(pool_b[:, :, 0])

        @pl.when(gz == nz - 1)
        def _():
            pool_b[:, :, 5] = jnp.zeros_like(pool_b[:, :, 5])

        @pl.when(gy == 0)
        def _():
            pool_b[:, :, :, 0:8, :] = jnp.zeros_like(pool_b[:, :, :, 0:8, :])

        @pl.when(gy == ny - 1)
        def _():
            pool_b[:, :, :, 16:24, :] = jnp.zeros_like(pool_b[:, :, :, 16:24, :])

        for k in range(27):
            im[0, 0:128, k * 128 : (k + 1) * 128] = tap(pool_b, 0, k // 9, k // 3 % 3, k % 3)
        swap_pool = plan(im.at[0, pl.ds(0, 128)], im.at[0, pl.ds(128, 128)], pair_send.at[0], pair_recv.at[0], other)

        @pl.when(core == 0)
        def _():
            swap_pool.start()

        loads[3].wait()
        pre = jnp.dot(im[0, 0:128, :], w1[...].reshape(3456, 256), preferred_element_type=F32)
        sig = 1.0 / (1.0 + jnp.exp(-pre))
        hidden = (pre * sig).astype(BF16)
        slope = sig * (1.0 + pre * (1.0 - sig))
        hb[1, 0:128, :] = hidden
        swap_hidden = plan(hb.at[1, pl.ds(0, 128)], hb.at[1, pl.ds(128, 128)], pair_send.at[1], pair_recv.at[1], other)

        @pl.when(core == 1)
        def _():
            swap_hidden.start()

        wide = hidden.astype(F32).reshape(4, 4, 8, 256)
        hid_b[0, 1:5, 1:5, 8:16, :] = wide[..., 0:128]
        hid_b[1, 1:5, 1:5, 8:16, :] = wide[..., 128:256]
        hid_xz = start_xz(hid_b, 1)

        for copy in cots:
            copy.wait_recv()

        @pl.when(gx == 0)
        def _():
            cp[0] = jnp.zeros_like(cp[0])
            zq[:, 0] = jnp.zeros_like(zq[:, 0])

        @pl.when(gx == nx - 1)
        def _():
            cp[9] = jnp.zeros_like(cp[9])
            zq[:, 9] = jnp.zeros_like(zq[:, 9])

        @pl.when(gy == 0)
        def _():
            cp[:, 0:8, :] = jnp.zeros_like(cp[:, 0:8, :])
            zq[:, :, 0:8, :] = jnp.zeros_like(zq[:, :, 0:8, :])

        @pl.when(gy == ny - 1)
        def _():
            cp[:, 136:144, :] = jnp.zeros_like(cp[:, 136:144, :])
            zq[:, :, 24:32, :] = jnp.zeros_like(zq[:, :, 24:32, :])

        @pl.when(gz == 0)
        def _():
            zq[0] = jnp.zeros_like(zq[0])

        @pl.when(gz == nz - 1)
        def _():
            zq[1] = jnp.zeros_like(zq[1])

        def swap_windows(x):
            rows, theirs = pl.ds(pl.multiple_of(x * 32, 32), 32), pl.ds(pl.multiple_of(128 + x * 32, 32), 32)
            return plan(im.at[1, rows], im.at[1, theirs], pair_send.at[3 + x], pair_recv.at[3 + x], other)

        def windows(x, carry):
            rows = pl.ds(pl.multiple_of(x * 32, 32), 32)
            for a in range(3):
                planes = pl.ds(2 * x + 2 - a, 2)
                sums = []
                for z in range(10):
                    columns = []
                    for y in range(4):
                        if z == 0:
                            value = zq[0, planes, pl.ds(7 + y, 8, stride=2), :]
                        elif z == 9:
                            value = zq[1, planes, pl.ds(7 + y, 8, stride=2), :]
                        else:
                            value = cp[planes, pl.ds(y * 8 + z - 1, 8, stride=16), :]
                        columns.append(value[0] + value[1])
                    sums.append([columns[2 - b] + columns[3 - b] for b in range(3)])
                for b in range(3):
                    for c in range(3):
                        k = 9 * a + 3 * b + c
                        value = jnp.concatenate(
                            [sums[2 * z + 2 - c][b] + sums[2 * z + 3 - c][b] for z in range(4)], axis=0
                        )
                        im[1, rows, k * 128 : (k + 1) * 128] = value.astype(BF16)

            @pl.when(core == 1)
            def _():
                swap_windows(x).start()

            return carry

        lax.fori_loop(0, 4, windows, 0)

        d_hidden = jnp.zeros((128, 256), F32)
        for k in range(27):
            d_hidden = d_hidden + lax.dot_general(
                im[1, 0:128, k * 128 : (k + 1) * 128], w2[k], (((1,), (1,)), ((), ())), preferred_element_type=F32
            )
        d_pre = (d_hidden * slope).astype(BF16)
        hb[0, 0:128, :] = d_pre
        swap_d_pre = plan(hb.at[0, pl.ds(0, 128)], hb.at[0, pl.ds(128, 128)], pair_send.at[2], pair_recv.at[2], other)

        @pl.when(core == 0)
        def _():
            swap_d_pre.start()

        def ring(axis, step):
            return at(2 * step, 0, 0) if axis == 0 else at(0, step, 0)

        def place(axis, step):
            return lax.rem(chip + (step + 4), 4) if axis == 0 else lax.rem(gy + (step + 4), 4)

        BOTH = [(h, i, d) for h in range(2) for i, d in enumerate((1, -1))]

        def block(h, i, step):
            return g.at[h, pl.ds(4 * i, 4), pl.ds(7 * place(h, step), 7)]

        def ring_start():
            opposite = {
                (h, i): remote(
                    block(h, i, 2), a1.at[h, i], rs_send.at[0, h, i], rs_recv.at[0, h, i], ring(h, d)
                )
                for h, i, d in BOTH
            }
            nearest = {
                (h, i): remote(
                    block(h, 1 - i, d), a2.at[h, i], rs_send.at[1, h, i], rs_recv.at[1, h, i], ring(h, d)
                )
                for h, i, d in BOTH
            }
            sent.extend([*opposite.values(), *nearest.values()])
            return opposite, nearest

        def ring_relay(opposite):
            relays = {}
            for h, i, d in BOTH:
                opposite[h, i].wait_recv()
                a3s[h, i] = (block(h, i, d)[...].astype(F32) + a1[h, i].astype(F32)).astype(BF16)
                relays[h, i] = remote(a3s.at[h, i], a3.at[h, i], rs_send.at[2, h, i], rs_recv.at[2, h, i], ring(h, d))
            sent.extend(relays.values())
            return relays

        def ring_end(nearest, relays):
            for h, i, d in BOTH:
                nearest[h, 1 - i].wait_recv()
                relays[h, i].wait_recv()
                total = block(h, i, 0)[...].astype(F32) + a2[h, 1 - i].astype(F32) + a3[h, i].astype(F32)
                r1[h, 4 * i : 4 * i + 4, 0:7] = total.astype(BF16)

        def scatter():
            copies = [[], []]
            for step in (2, 1, 3):
                for h in range(2):
                    axis = 1 - h
                    copies[h].append(
                        remote(
                            r1.at[h, :, pl.ds(2 * place(axis, step), 2)], gb.at[h, step - 1],
                            rs_send.at[3 + step - 1, h, 0], rs_recv.at[3 + step - 1, h, 0], ring(axis, step),
                        )
                    )
            sent.extend(copies[0] + copies[1])
            return copies

        def add_up(copies, h):
            for copy in copies[h]:
                copy.wait_recv()
            total = r1[h, :, pl.ds(2 * place(1 - h, 0), 2)].astype(F32)
            for step in range(3):
                total = total + gb[h, step].astype(F32)
            r2[:, h] = total.astype(BF16)

        wide = d_pre.astype(F32).reshape(4, 4, 8, 256)
        dp_b[0, 1:5, 1:5, 8:16, :] = wide[..., 0:128]
        dp_b[1, 1:5, 1:5, 8:16, :] = wide[..., 128:256]
        dp_xz = start_xz(dp_b, 2)
        hid_y = start_y(hid_b, hid_s, hid_r, 1, hid_xz)

        g[:, :, 27] = jnp.zeros((2, 8, 16, 128), BF16)

        @pl.when(core == 0)
        def _():
            swap_hidden.wait_recv()
            for x in range(4):
                swap_windows(x).wait_recv()
            right = hb[1]
            for k in range(27):
                value = lax.dot_general(
                    im[1, :, k * 128 : (k + 1) * 128], right, (((0,), (0,)), ((), ())), preferred_element_type=F32
                ).astype(BF16)
                value = value.reshape(8, 16, 256)
                g[0, :, k] = value[..., 0:128]
                g[1, :, k] = value[..., 128:256]

        @pl.when(core == 1)
        def _():
            swap_pool.wait_recv()
            swap_d_pre.wait_recv()
            left = hb[0].astype(F32).T.astype(BF16)
            for k in range(27):
                value = jnp.dot(left, im[0, :, k * 128 : (k + 1) * 128], preferred_element_type=F32).astype(BF16)
                value = value.reshape(8, 2, 16, 128)
                g[0, :, k] = value[:, 0]
                g[1, :, k] = value[:, 1]

        opposite, nearest = ring_start()
        dp_y = start_y(dp_b, dp_s, dp_r, 2, dp_xz)
        relays = ring_relay(opposite)


        finish_y(hid_b, hid_r, hid_y)
        for k in range(27):
            for h in range(2):
                hi[:, k * 256 + h * 128 : k * 256 + (h + 1) * 128] = tap(hid_b, h, k // 9, k // 3 % 3, k % 3)

        for parity in range(8):
            pa, pb, pc = parity // 4, parity // 2 % 2, parity % 2
            total = jnp.zeros((128, 128), F32)
            for side in range(4):
                k = 9 * (pa + side // 2) + 3 * (pb + side % 2) + pc
                total = total + jnp.dot(hi[:, k * 256 : k * 256 + 512], wc[parity, side], preferred_element_type=F32)
            total = total.reshape(4, 4, 8, 128)
            for z in range(4):
                ob[:, pa, pl.ds(pb * 8 + 2 * z + pc, 8, stride=16), :] = total[:, z]
        for x in range(8):
            out_v[x] = (field_v[x].astype(F32) + ob[x // 2, x % 2]).astype(BF16)

        out_copy = pltpu.make_async_copy(out_v, out_hbm, out_sem.at[0])
        out_copy.start()
        drain()

        @pl.when(core == 0)
        def _():
            swap_pool.wait_send()
            swap_d_pre.wait_send()

        @pl.when(core == 1)
        def _():
            swap_hidden.wait_send()
            for x in range(4):
                swap_windows(x).wait_send()

        r1[:, :, 7] = jnp.zeros((2, 8, 16, 128), BF16)
        ring_end(nearest, relays)
        second = scatter()

        for h in range(2):
            add_up(second, h)

        ups = []
        for d in range(1, nz):
            ups.append(
                remote(
                    r2.at[lax.rem(gz + d, nz)], zb.at[gz], z_send.at[d - 1], z_recv.at[d - 1], at(0, 0, d)
                )
            )
        sent.extend(ups)
        zb[gz] = r2[gz]

        finish_y(dp_b, dp_r, dp_y)
        for k in range(27):
            for h in range(2):
                di[:, k * 256 + h * 128 : k * 256 + (h + 1) * 128] = tap(dp_b, h, k // 9, k // 3 % 3, k % 3)

        total = jnp.zeros((128, 128), F32)
        for k in range(27):
            total = total + lax.dot_general(
                di[:, k * 256 : (k + 1) * 256], w1[26 - k], (((1,), (1,)), ((), ())), preferred_element_type=F32
            )
        total = (total * 0.125).reshape(4, 4, 8, 128)
        for z in range(4):
            for j in range(4):
                fg[:, pl.ds(j // 2 * 8 + 2 * z + j % 2, 8, stride=16), :] = total[:, z]
        for x in range(8):
            grad_v[x] = (cot_v[x].astype(F32) + fg[x // 2]).astype(BF16)

        grad_copy = pltpu.make_async_copy(grad_v, grad_hbm, out_sem.at[1])
        grad_copy.start()
        drain()
        for copy in ups:
            copy.wait_recv()
        total = zb[0].astype(F32)
        for j in range(1, nz):
            total = total + zb[j].astype(F32)
        scale = jnp.where(core == 0, F32(1.0 / math.sqrt(cells)), F32(1.0 / math.sqrt(cells / 8.0)))
        mine = chip * ny + gy
        ag[core, mine] = (total * scale).astype(BF16)

        steps = sorted(((i, j) for i in range(chips) for j in range(ny)), key=hops)
        swap = 1 - 2 * core
        drain()

        def spread_to(n, cross):
            dx, dy = steps[n]
            x, y, z = at(2 * dx, dy, 0)
            i = n + 16 * cross
            return remote(
                ag.at[core, mine], ag.at[core, mine], ag_send.at[i], ag_recv.at[i], (x + swap * cross, y, z)
            )

        gathers = {}
        for n in reversed(range(1, 16)):
            gathers[n, 0] = spread_to(n, 0)
            if hops(steps[n]) > 2:
                gathers[n, 1] = spread_to(n, 1)
        sent.extend(gathers.values())
        for n, (dx, dy) in enumerate(steps):
            if hops(steps[n]) <= 2:
                if n > 0:
                    gathers[n, 0].wait_recv()
                came = lax.rem(chip + chips - dx, chips) * ny + lax.rem(gy + ny - dy, ny)
                gathers[n, 2] = remote(ag.at[core, came], ag.at[core, came], fwd_send.at[n], fwd_recv.at[n], other)
                sent.append(gathers[n, 2])
        out_copy.wait()
        grad_copy.wait()
        for (n, way), copy in gathers.items():
            if n == 0 or hops(steps[n]) > 2 or way == 2:
                copy.wait_recv()
        drain()

    return kernel


def finish(out_in, grad_in, ag, out_ref, grad_ref, fine_ref, coarse_ref):
    out_ref[...] = out_in[...]
    grad_ref[...] = grad_in[...]
    for k in range(27):
        j = k % 7
        for h in range(2):
            src = k // 7 * 4 + j // 2 if h == 0 else j // 2 * 4 + k // 7
            fine_ref[k, :, h * 128 : (h + 1) * 128] = ag[0, src, h, j % 2].astype(F32)
            coarse_ref[k, 16 * h : 16 * h + 16, :] = ag[1, src, h, j % 2].astype(F32)


def solution(mesh):
    sizes = (mesh.shape["gx"], mesh.shape["gy"], mesh.shape["gz"])
    dma = pltpu.SemaphoreType.DMA

    def local(field, coarse_weight, fine_weight, cotangent):
        v = pltpu.VMEM
        scratch = [
            v((8, 128, 128), BF16), v((8, 128, 128), BF16), v((27, 128, 256), BF16), v((27, 256, 128), BF16),
            v((8, 4, 512, 128), BF16), v((8, 128, 128), BF16), v((8, 128, 128), BF16),
            v((10, 144, 128), F32), v((2, 8, 16, 128), F32), v((2, 10, 32, 128), F32), v((4, 64, 128), F32),
            v((1, 6, 6, 24, 128), F32),
            v((2, 6, 6, 24, 128), F32), v((2, 2, 40, 128), F32), v((2, 2, 40, 128), F32),
            v((2, 6, 6, 24, 128), F32), v((2, 2, 40, 128), F32), v((2, 2, 40, 128), F32),
            v((2, 256, 3456), BF16), v((2, 256, 256), BF16), v((128, 6912), BF16), v((128, 6912), BF16),
            v((4, 2, 128, 128), F32), v((4, 128, 128), F32),
            v((2, 8, 28, 16, 128), BF16),
            v((2, 2, 4, 7, 16, 128), BF16), v((2, 2, 4, 7, 16, 128), BF16),
            v((2, 2, 4, 7, 16, 128), BF16), v((2, 2, 4, 7, 16, 128), BF16),
            v((2, 8, 8, 16, 128), BF16), v((2, 3, 8, 2, 16, 128), BF16),
            v((8, 2, 2, 16, 128), BF16), v((8, 2, 2, 16, 128), BF16),
            dma((4,)), dma((2,)), dma((4, 26)), dma((4, 26)), dma((7,)), dma((7,)), dma((16,)), dma((16,)),
            dma((6, 2, 2)), dma((6, 2, 2)), dma((7,)), dma((7,)), dma((32,)), dma((32,)),
        ]
        anywhere = pl.BlockSpec(memory_space=pl.ANY)
        inside = pl.BlockSpec(memory_space=pltpu.VMEM)
        cells = jax.ShapeDtypeStruct((8, 128, 128), BF16)
        output, field_grad, terms = pl.pallas_call(
            make_kernel(sizes),
            out_shape=(cells, cells, jax.ShapeDtypeStruct((2, 16, 2, 2, 16, 128), BF16)),
            in_specs=[anywhere] * 4,
            out_specs=(anywhere, anywhere, inside),
            scratch_shapes=scratch,
            compiler_params=pltpu.CompilerParams(
                collective_id=0, has_side_effects=True, vmem_limit_bytes=56 * 1024 * 1024
            ),
        )(field.reshape(8, 128, 128), coarse_weight, fine_weight, cotangent.reshape(8, 128, 128))
        output, field_grad, fine, coarse = pl.pallas_call(
            finish,
            out_shape=(
                cells,
                cells,
                jax.ShapeDtypeStruct((27, 16, 256), F32),
                jax.ShapeDtypeStruct((27, 32, 128), F32),
            ),
            in_specs=[inside] * 3,
            out_specs=(inside,) * 4,
        )(output, field_grad, terms)
        return (
            output.reshape(8, 16, 8, 128),
            field_grad.reshape(8, 16, 8, 128),
            fine.transpose(0, 2, 1),
            coarse.transpose(0, 2, 1),
        )

    placed = (P("gx", "gy", "gz", None), P(), P(), P("gx", "gy", "gz", None))
    return jax.shard_map(
        local,
        mesh=mesh,
        in_specs=placed,
        out_specs=(
            P("gx", "gy", "gz", None),
            P("gx", "gy", "gz", None),
            P(None, None, "gz"),
            P(None, None, "gz"),
        ),
        check_vma=False,
    )
```

```python
import math

import jax
import jax.numpy as jnp
from jax import lax
from jax.experimental import pallas as pl
from jax.experimental.pallas import tpu as pltpu
from jax.sharding import PartitionSpec as P

MESH = pl.DeviceIdType.MESH
F32 = jnp.float32
BF16 = jnp.bfloat16

SIDES = (-1, 0, 1)
EIGHT = [(i, j) for i in SIDES for j in SIDES if (i, j) != (0, 0)]
NEAR = sorted(((i, j, k) for i in SIDES for j in SIDES for k in SIDES if (i, j, k) != (0, 0, 0)), key=lambda p: -sum(map(abs, p)))
PAIRS = ((0,), (1, 2), (0, 1), (2,))


def from_side(step, length):
    return pl.ds(1, length) if step == 0 else pl.ds(length if step > 0 else 1, 1)


def to_side(step, length):
    return pl.ds(1, length) if step == 0 else pl.ds(0 if step > 0 else length + 1, 1)


def make_kernel(sizes):
    nx, ny, nz = sizes
    chips = nx // 2
    cells = 1024 * nx * ny * nz

    def kernel(
        field_hbm, w1_hbm, w2_hbm, cot_hbm,
        out_hbm, grad_hbm, ag,
        field_v, cot_v, w1, w2, wc, out_v, grad_v,
        cp, zs, zq, tmp, pool_b, hid_b, hid_s, hid_r, dp_b, dp_s, dp_r,
        im, hb, hi, di, ob, fg,
        g, a1, a2, a3s, a3, r1, gb, r2, zb,
        in_sem, out_sem, halo_send, halo_recv, pair_send, pair_recv, fwd_send, fwd_recv, rs_send, rs_recv, z_send, z_recv, ag_send, ag_recv,
    ):
        gx, gy, gz = lax.axis_index("gx"), lax.axis_index("gy"), lax.axis_index("gz")
        core = lax.rem(gx, 2)
        chip = gx // 2

        def at(dx, dy, dz):
            return (
                lax.rem(gx + (dx + nx), nx),
                lax.rem(gy + (dy + ny), ny),
                lax.rem(gz + (dz + nz), nz),
            )

        def plan(src, dst, send, recv, device):
            return pltpu.make_async_remote_copy(
                src_ref=src, dst_ref=dst, send_sem=send, recv_sem=recv, device_id=device, device_id_type=MESH
            )

        def remote(*where):
            copy = plan(*where)
            copy.start()
            return copy

        other = (gx + 1 - 2 * core, gy, gz)
        sent = []

        def drain():
            for copy in sent:
                copy.wait_send()
            sent.clear()

        def hops(p):
            return min(p[0], chips - p[0]) + min(p[1], ny - p[1])

        loads = [
            pltpu.make_async_copy(src, dst, in_sem.at[i])
            for i, (src, dst) in enumerate(
                ((field_hbm, field_v), (cot_hbm, cot_v), (w2_hbm, w2), (w1_hbm, w1))
            )
        ]
        for load in loads:
            load.start()

        partners = {(i % nx, j % ny, k % nz) for i, j, k in NEAR}
        partners |= {(0, 0, k) for k in range(1, nz)}
        partners |= {(2 * i, j, 0) for i in range(chips) for j in range(ny) if (i, j) != (0, 0)}
        barrier = pltpu.get_barrier_semaphore()
        for step in sorted(partners):
            pl.semaphore_signal(barrier, inc=1, device_id=at(*step), device_id_type=MESH)

        loads[0].wait()
        for x in range(4):
            pair = field_v[2 * x].astype(F32) + field_v[2 * x + 1].astype(F32)
            pair = pair.reshape(8, 2, 8, 128)
            tmp[x] = (pair[:, 0] + pair[:, 1]).reshape(64, 128)
        for z in range(4):
            total = tmp[:, pl.ds(2 * z, 8, stride=8), :] + tmp[:, pl.ds(2 * z + 1, 8, stride=8), :]
            pool_b[0, 1:5, 1 + z, 8:16, :] = (total * 0.125).astype(BF16).astype(F32)
        loads[1].wait()
        for x in range(8):
            cp[1 + x, 8:136, :] = cot_v[x].astype(F32)
        zs[0] = cp[1:9, pl.ds(8, 16, stride=8), :]
        zs[1] = cp[1:9, pl.ds(15, 16, stride=8), :]

        pl.semaphore_wait(barrier, len(partners))

        def start_xz(buf, e):
            copies = []
            for i, (dx, dz) in enumerate(EIGHT):
                copies.append(
                    remote(
                        buf.at[:, from_side(dx, 4), from_side(dz, 4), pl.ds(8, 8), :],
                        buf.at[:, to_side(dx, 4), to_side(dz, 4), pl.ds(8, 8), :],
                        halo_send.at[e, i], halo_recv.at[e, i], at(dx, 0, dz),
                    )
                )
            sent.extend(copies)
            return copies

        def start_y(buf, s, r, e, copies):
            for copy in copies:
                copy.wait_recv()

            @pl.when(gx == 0)
            def _():
                buf[:, 0, :, 8:16, :] = jnp.zeros_like(buf[:, 0, :, 8:16, :])

            @pl.when(gx == nx - 1)
            def _():
                buf[:, 5, :, 8:16, :] = jnp.zeros_like(buf[:, 5, :, 8:16, :])

            @pl.when(gz == 0)
            def _():
                buf[:, :, 0, 8:16, :] = jnp.zeros_like(buf[:, :, 0, 8:16, :])

            @pl.when(gz == nz - 1)
            def _():
                buf[:, :, 5, 8:16, :] = jnp.zeros_like(buf[:, :, 5, 8:16, :])

            flat = buf.reshape(buf.shape[0], 864, 128)
            for h in range(buf.shape[0]):
                s[0, h, 0:36, :] = flat[h, pl.ds(8, 36, stride=24), :]
                s[1, h, 0:36, :] = flat[h, pl.ds(15, 36, stride=24), :]
            below = remote(s.at[0], r.at[1], halo_send.at[e, 8], halo_recv.at[e, 8], at(0, -1, 0))
            above = remote(s.at[1], r.at[0], halo_send.at[e, 9], halo_recv.at[e, 9], at(0, 1, 0))
            sent.extend((below, above))
            return (above, below)

        def finish_y(buf, r, copies):
            for copy in copies:
                copy.wait_recv()

            @pl.when(gy == 0)
            def _():
                r[0] = jnp.zeros_like(r[0])

            @pl.when(gy == ny - 1)
            def _():
                r[1] = jnp.zeros_like(r[1])

            flat = buf.reshape(buf.shape[0], 864, 128)
            for h in range(buf.shape[0]):
                flat[h, pl.ds(7, 36, stride=24), :] = r[0, h, 0:36, :]
                flat[h, pl.ds(16, 36, stride=24), :] = r[1, h, 0:36, :]

        def tap(buf, h, a, b, c):
            return buf[h, a : a + 4, c : c + 4, 7 + b : 15 + b, :].reshape(128, 128).astype(BF16)

        def send_pool(i):
            dx, dy, dz = NEAR[i]
            return remote(
                pool_b.at[:, from_side(dx, 4), from_side(dz, 4), pl.ds(8, 8), :],
                pool_b.at[:, to_side(dx, 4), to_side(dz, 4), pl.ds(8 - 8 * dy, 8), :],
                halo_send.at[0, i], halo_recv.at[0, i], at(dx, dy, dz),
            )

        def send_cot(i):
            dx, dy, dz = NEAR[i]
            if dz == 0:
                sy = pl.ds(8, 128) if dy == 0 else pl.ds(128 if dy > 0 else 8, 8)
                ty = pl.ds(8, 128) if dy == 0 else pl.ds(0 if dy > 0 else 136, 8)
                src, dst = cp.at[from_side(dx, 8), sy, :], cp.at[to_side(dx, 8), ty, :]
            else:
                sx = pl.ds(0, 8) if dx == 0 else pl.ds(7 if dx > 0 else 0, 1)
                sy = pl.ds(0, 16) if dy == 0 else pl.ds(8 if dy > 0 else 0, 8)
                ty = pl.ds(8, 16) if dy == 0 else pl.ds(0 if dy > 0 else 24, 8)
                src = zs.at[1 if dz > 0 else 0, sx, sy, :]
                dst = zq.at[0 if dz > 0 else 1, to_side(dx, 8), ty, :]
            return remote(src, dst, halo_send.at[3, i], halo_recv.at[3, i], at(dx, dy, dz))

        pools, cots = [], []
        faces = [i for i in range(26) if sum(map(abs, NEAR[i])) == 1]
        for i in faces:
            cots.append(send_cot(i))
        for i in range(26):
            pools.append(send_pool(i))
            if i not in faces:
                cots.append(send_cot(i))
        sent.extend(pools + cots)

        loads[2].wait()

        def combine(i, carry):
            rows = pl.ds(pl.multiple_of(i * 16, 16), 16)
            low = pl.ds(pl.multiple_of(i * 16, 16), 16)
            high = pl.ds(pl.multiple_of(256 + i * 16, 16), 16)

            def spread(parts):
                return (parts[0], parts[1] + parts[2], parts[0] + parts[1], parts[2])

            by_ab = [[spread([w2[9 * a + 3 * b + c, rows, :].astype(F32) for c in range(3)]) for b in range(3)] for a in range(3)]
            by_a = [[spread([by_ab[a][b][c] for b in range(3)]) for c in range(4)] for a in range(3)]
            for b in range(4):
                for c in range(4):
                    for a, value in enumerate(spread([by_a[a][c][b] for a in range(3)])):
                        parity = (a // 2) * 4 + (b // 2) * 2 + c // 2
                        wc[parity, (a % 2) * 2 + b % 2, high if c % 2 else low, :] = value.astype(BF16)
            return carry

        lax.fori_loop(0, 16, combine, 0)

        for copy in pools:
            copy.wait_recv()

        @pl.when(gx == 0)
        def _():
            pool_b[:, 0] = jnp.zeros_like(pool_b[:, 0])

        @pl.when(gx == nx - 1)
        def _():
            pool_b[:, 5] = jnp.zeros_like(pool_b[:, 5])

        @pl.when(gz == 0)
        def _():
            pool_b[:, :, 0] = jnp.zeros_like(pool_b[:, :, 0])

        @pl.when(gz == nz - 1)
        def _():
            pool_b[:, :, 5] = jnp.zeros_like(pool_b[:, :, 5])

        @pl.when(gy == 0)
        def _():
            pool_b[:, :, :, 0:8, :] = jnp.zeros_like(pool_b[:, :, :, 0:8, :])

        @pl.when(gy == ny - 1)
        def _():
            pool_b[:, :, :, 16:24, :] = jnp.zeros_like(pool_b[:, :, :, 16:24, :])

        for k in range(27):
            im[0, 0:128, k * 128 : (k + 1) * 128] = tap(pool_b, 0, k // 9, k // 3 % 3, k % 3)
        swap_pool = plan(im.at[0, pl.ds(0, 128)], im.at[0, pl.ds(128, 128)], pair_send.at[0], pair_recv.at[0], other)

        @pl.when(core == 0)
        def _():
            swap_pool.start()

        loads[3].wait()
        pre = jnp.dot(im[0, 0:128, :], w1[...].reshape(3456, 256), preferred_element_type=F32)
        sig = 1.0 / (1.0 + jnp.exp(-pre))
        hidden = (pre * sig).astype(BF16)
        slope = sig * (1.0 + pre * (1.0 - sig))
        hb[1, 0:128, :] = hidden
        swap_hidden = plan(hb.at[1, pl.ds(0, 128)], hb.at[1, pl.ds(128, 128)], pair_send.at[1], pair_recv.at[1], other)

        @pl.when(core == 1)
        def _():
            swap_hidden.start()

        wide = hidden.astype(F32).reshape(4, 4, 8, 256)
        hid_b[0, 1:5, 1:5, 8:16, :] = wide[..., 0:128]
        hid_b[1, 1:5, 1:5, 8:16, :] = wide[..., 128:256]

        for copy in cots:
            copy.wait_recv()

        @pl.when(gx == 0)
        def _():
            cp[0] = jnp.zeros_like(cp[0])
            zq[:, 0] = jnp.zeros_like(zq[:, 0])

        @pl.when(gx == nx - 1)
        def _():
            cp[9] = jnp.zeros_like(cp[9])
            zq[:, 9] = jnp.zeros_like(zq[:, 9])

        @pl.when(gy == 0)
        def _():
            cp[:, 0:8, :] = jnp.zeros_like(cp[:, 0:8, :])
            zq[:, :, 0:8, :] = jnp.zeros_like(zq[:, :, 0:8, :])

        @pl.when(gy == ny - 1)
        def _():
            cp[:, 136:144, :] = jnp.zeros_like(cp[:, 136:144, :])
            zq[:, :, 24:32, :] = jnp.zeros_like(zq[:, :, 24:32, :])

        @pl.when(gz == 0)
        def _():
            zq[0] = jnp.zeros_like(zq[0])

        @pl.when(gz == nz - 1)
        def _():
            zq[1] = jnp.zeros_like(zq[1])

        def swap_windows(x):
            rows, theirs = pl.ds(pl.multiple_of(x * 32, 32), 32), pl.ds(pl.multiple_of(128 + x * 32, 32), 32)
            return plan(im.at[1, rows], im.at[1, theirs], pair_send.at[3 + x], pair_recv.at[3 + x], other)

        def windows(x, carry):
            rows = pl.ds(pl.multiple_of(x * 32, 32), 32)
            for a in range(3):
                planes = pl.ds(2 * x + 2 - a, 2)
                sums = []
                for z in range(10):
                    columns = []
                    for y in range(4):
                        if z == 0:
                            value = zq[0, planes, pl.ds(7 + y, 8, stride=2), :]
                        elif z == 9:
                            value = zq[1, planes, pl.ds(7 + y, 8, stride=2), :]
                        else:
                            value = cp[planes, pl.ds(y * 8 + z - 1, 8, stride=16), :]
                        columns.append(value[0] + value[1])
                    sums.append([columns[2 - b] + columns[3 - b] for b in range(3)])
                for b in range(3):
                    for c in range(3):
                        k = 9 * a + 3 * b + c
                        value = jnp.concatenate(
                            [sums[2 * z + 2 - c][b] + sums[2 * z + 3 - c][b] for z in range(4)], axis=0
                        )
                        im[1, rows, k * 128 : (k + 1) * 128] = value.astype(BF16)

            @pl.when(core == 1)
            def _():
                swap_windows(x).start()

            return carry

        lax.fori_loop(0, 4, windows, 0)

        d_hidden = jnp.zeros((128, 256), F32)
        for k in range(27):
            d_hidden = d_hidden + lax.dot_general(
                im[1, 0:128, k * 128 : (k + 1) * 128], w2[k], (((1,), (1,)), ((), ())), preferred_element_type=F32
            )
        d_pre = (d_hidden * slope).astype(BF16)
        hb[0, 0:128, :] = d_pre
        swap_d_pre = plan(hb.at[0, pl.ds(0, 128)], hb.at[0, pl.ds(128, 128)], pair_send.at[2], pair_recv.at[2], other)

        @pl.when(core == 0)
        def _():
            swap_d_pre.start()

        def ring(axis, step):
            return at(2 * step, 0, 0) if axis == 0 else at(0, step, 0)

        def place(axis, step):
            return lax.rem(chip + (step + 4), 4) if axis == 0 else lax.rem(gy + (step + 4), 4)

        BOTH = [(h, i, d) for h in range(2) for i, d in enumerate((1, -1))]

        def block(h, i, step):
            return g.at[h, pl.ds(4 * i, 4), pl.ds(7 * place(h, step), 7)]

        def ring_start():
            opposite = {
                (h, i): remote(
                    block(h, i, 2), a1.at[h, i], rs_send.at[0, h, i], rs_recv.at[0, h, i], ring(h, d)
                )
                for h, i, d in BOTH
            }
            nearest = {
                (h, i): remote(
                    block(h, 1 - i, d), a2.at[h, i], rs_send.at[1, h, i], rs_recv.at[1, h, i], ring(h, d)
                )
                for h, i, d in BOTH
            }
            sent.extend([*opposite.values(), *nearest.values()])
            return opposite, nearest

        def ring_relay(opposite):
            relays = {}
            for h, i, d in BOTH:
                opposite[h, i].wait_recv()
                a3s[h, i] = (block(h, i, d)[...].astype(F32) + a1[h, i].astype(F32)).astype(BF16)
                relays[h, i] = remote(a3s.at[h, i], a3.at[h, i], rs_send.at[2, h, i], rs_recv.at[2, h, i], ring(h, d))
            sent.extend(relays.values())
            return relays

        def ring_end(nearest, relays):
            for h, i, d in BOTH:
                nearest[h, 1 - i].wait_recv()
                relays[h, i].wait_recv()
                total = block(h, i, 0)[...].astype(F32) + a2[h, 1 - i].astype(F32) + a3[h, i].astype(F32)
                r1[h, 4 * i : 4 * i + 4, 0:7] = total.astype(BF16)

        def scatter():
            copies = [[], []]
            for step in (2, 1, 3):
                for h in range(2):
                    axis = 1 - h
                    copies[h].append(
                        remote(
                            r1.at[h, :, pl.ds(2 * place(axis, step), 2)], gb.at[h, step - 1],
                            rs_send.at[3 + step - 1, h, 0], rs_recv.at[3 + step - 1, h, 0], ring(axis, step),
                        )
                    )
            sent.extend(copies[0] + copies[1])
            return copies

        def add_up(copies, h):
            for copy in copies[h]:
                copy.wait_recv()
            total = r1[h, :, pl.ds(2 * place(1 - h, 0), 2)].astype(F32)
            for step in range(3):
                total = total + gb[h, step].astype(F32)
            r2[:, h] = total.astype(BF16)

        wide = d_pre.astype(F32).reshape(4, 4, 8, 256)
        dp_b[0, 1:5, 1:5, 8:16, :] = wide[..., 0:128]
        dp_b[1, 1:5, 1:5, 8:16, :] = wide[..., 128:256]

        g[:, :, 27] = jnp.zeros((2, 8, 16, 128), BF16)

        @pl.when(core == 0)
        def _():
            swap_hidden.wait_recv()
            for x in range(4):
                swap_windows(x).wait_recv()
            right = hb[1]
            for k in range(27):
                value = lax.dot_general(
                    im[1, :, k * 128 : (k + 1) * 128], right, (((0,), (0,)), ((), ())), preferred_element_type=F32
                ).astype(BF16)
                value = value.reshape(8, 16, 256)
                g[0, :, k] = value[..., 0:128]
                g[1, :, k] = value[..., 128:256]

        @pl.when(core == 1)
        def _():
            swap_pool.wait_recv()
            swap_d_pre.wait_recv()
            left = hb[0].astype(F32).T.astype(BF16)
            for k in range(27):
                value = jnp.dot(left, im[0, :, k * 128 : (k + 1) * 128], preferred_element_type=F32).astype(BF16)
                value = value.reshape(8, 2, 16, 128)
                g[0, :, k] = value[:, 0]
                g[1, :, k] = value[:, 1]

        opposite, nearest = ring_start()
        hid_xz = start_xz(hid_b, 1)
        dp_xz = start_xz(dp_b, 2)
        relays = ring_relay(opposite)
        hid_y = start_y(hid_b, hid_s, hid_r, 1, hid_xz)
        dp_y = start_y(dp_b, dp_s, dp_r, 2, dp_xz)

        r1[:, :, 7] = jnp.zeros((2, 8, 16, 128), BF16)
        ring_end(nearest, relays)
        second = scatter()


        finish_y(hid_b, hid_r, hid_y)
        for k in range(27):
            for h in range(2):
                hi[:, k * 256 + h * 128 : k * 256 + (h + 1) * 128] = tap(hid_b, h, k // 9, k // 3 % 3, k % 3)

        def conv(parity):
            pa, pb, pc = parity // 4, parity // 2 % 2, parity % 2
            total = jnp.zeros((128, 128), F32)
            for side in range(4):
                k = 9 * (pa + side // 2) + 3 * (pb + side % 2) + pc
                total = total + jnp.dot(hi[:, k * 256 : k * 256 + 512], wc[parity, side], preferred_element_type=F32)
            total = total.reshape(4, 4, 8, 128)
            for z in range(4):
                ob[:, pa, pl.ds(pb * 8 + 2 * z + pc, 8, stride=16), :] = total[:, z]

        for parity in range(4):
            conv(parity)

        for h in range(2):
            add_up(second, h)

        ups = []
        for d in sorted(range(1, nz), key=lambda d: -min(d, nz - d)):
            ups.append(
                remote(
                    r2.at[lax.rem(gz + d, nz)], zb.at[gz], z_send.at[d - 1], z_recv.at[d - 1], at(0, 0, d)
                )
            )
        sent.extend(ups)
        zb[gz] = r2[gz]

        for parity in range(4, 8):
            conv(parity)
        for x in range(8):
            out_v[x] = (field_v[x].astype(F32) + ob[x // 2, x % 2]).astype(BF16)

        out_copy = pltpu.make_async_copy(out_v, out_hbm, out_sem.at[0])
        out_copy.start()
        drain()

        @pl.when(core == 0)
        def _():
            swap_pool.wait_send()
            swap_d_pre.wait_send()

        @pl.when(core == 1)
        def _():
            swap_hidden.wait_send()
            for x in range(4):
                swap_windows(x).wait_send()


        for copy in reversed(ups):
            copy.wait_recv()
        total = zb[0].astype(F32)
        for j in range(1, nz):
            total = total + zb[j].astype(F32)
        scale = jnp.where(core == 0, F32(1.0 / math.sqrt(cells)), F32(1.0 / math.sqrt(cells / 8.0)))
        mine = chip * ny + gy
        ag[core, mine] = (total * scale).astype(BF16)

        steps = sorted(((i, j) for i in range(chips) for j in range(ny)), key=hops)

        gathers = {}
        for n in reversed(range(1, 16)):
            dx, dy = steps[n]
            gathers[n] = remote(ag.at[core, mine], ag.at[core, mine], ag_send.at[n], ag_recv.at[n], at(2 * dx, dy, 0))
        sent.extend(gathers.values())

        finish_y(dp_b, dp_r, dp_y)
        for k in range(27):
            for h in range(2):
                di[:, k * 256 + h * 128 : k * 256 + (h + 1) * 128] = tap(dp_b, h, k // 9, k // 3 % 3, k % 3)

        total = jnp.zeros((128, 128), F32)
        for k in range(27):
            total = total + lax.dot_general(
                di[:, k * 256 : (k + 1) * 256], w1[26 - k], (((1,), (1,)), ((), ())), preferred_element_type=F32
            )
        total = (total * 0.125).reshape(4, 4, 8, 128)
        for z in range(4):
            for j in range(4):
                fg[:, pl.ds(j // 2 * 8 + 2 * z + j % 2, 8, stride=16), :] = total[:, z]
        for x in range(8):
            grad_v[x] = (cot_v[x].astype(F32) + fg[x // 2]).astype(BF16)

        grad_copy = pltpu.make_async_copy(grad_v, grad_hbm, out_sem.at[1])
        grad_copy.start()
        drain()

        forwards = []
        for n, (dx, dy) in enumerate(steps):
            if n > 0:
                gathers[n].wait_recv()
            came = lax.rem(chip + chips - dx, chips) * ny + lax.rem(gy + ny - dy, ny)
            forwards.append(remote(ag.at[core, came], ag.at[core, came], fwd_send.at[n], fwd_recv.at[n], other))
        sent.extend(forwards)
        out_copy.wait()
        grad_copy.wait()
        for copy in forwards:
            copy.wait_recv()
        drain()

    return kernel


def finish(out_in, grad_in, ag, out_ref, grad_ref, fine_ref, coarse_ref):
    out_ref[...] = out_in[...]
    grad_ref[...] = grad_in[...]
    for k in range(27):
        j = k % 7
        for h in range(2):
            src = k // 7 * 4 + j // 2 if h == 0 else j // 2 * 4 + k // 7
            fine_ref[k, :, h * 128 : (h + 1) * 128] = ag[0, src, h, j % 2].astype(F32)
            coarse_ref[k, 16 * h : 16 * h + 16, :] = ag[1, src, h, j % 2].astype(F32)


def solution(mesh):
    sizes = (mesh.shape["gx"], mesh.shape["gy"], mesh.shape["gz"])
    dma = pltpu.SemaphoreType.DMA

    def local(field, coarse_weight, fine_weight, cotangent):
        v = pltpu.VMEM
        scratch = [
            v((8, 128, 128), BF16), v((8, 128, 128), BF16), v((27, 128, 256), BF16), v((27, 256, 128), BF16),
            v((8, 4, 512, 128), BF16), v((8, 128, 128), BF16), v((8, 128, 128), BF16),
            v((10, 144, 128), F32), v((2, 8, 16, 128), F32), v((2, 10, 32, 128), F32), v((4, 64, 128), F32),
            v((1, 6, 6, 24, 128), F32),
            v((2, 6, 6, 24, 128), F32), v((2, 2, 40, 128), F32), v((2, 2, 40, 128), F32),
            v((2, 6, 6, 24, 128), F32), v((2, 2, 40, 128), F32), v((2, 2, 40, 128), F32),
            v((2, 256, 3456), BF16), v((2, 256, 256), BF16), v((128, 6912), BF16), v((128, 6912), BF16),
            v((4, 2, 128, 128), F32), v((4, 128, 128), F32),
            v((2, 8, 28, 16, 128), BF16),
            v((2, 2, 4, 7, 16, 128), BF16), v((2, 2, 4, 7, 16, 128), BF16),
            v((2, 2, 4, 7, 16, 128), BF16), v((2, 2, 4, 7, 16, 128), BF16),
            v((2, 8, 8, 16, 128), BF16), v((2, 3, 8, 2, 16, 128), BF16),
            v((8, 2, 2, 16, 128), BF16), v((8, 2, 2, 16, 128), BF16),
            dma((4,)), dma((2,)), dma((4, 26)), dma((4, 26)), dma((7,)), dma((7,)), dma((16,)), dma((16,)),
            dma((6, 2, 2)), dma((6, 2, 2)), dma((7,)), dma((7,)), dma((16,)), dma((16,)),
        ]
        anywhere = pl.BlockSpec(memory_space=pl.ANY)
        inside = pl.BlockSpec(memory_space=pltpu.VMEM)
        cells = jax.ShapeDtypeStruct((8, 128, 128), BF16)
        output, field_grad, terms = pl.pallas_call(
            make_kernel(sizes),
            out_shape=(cells, cells, jax.ShapeDtypeStruct((2, 16, 2, 2, 16, 128), BF16)),
            in_specs=[anywhere] * 4,
            out_specs=(anywhere, anywhere, inside),
            scratch_shapes=scratch,
            compiler_params=pltpu.CompilerParams(
                collective_id=0, has_side_effects=True, vmem_limit_bytes=56 * 1024 * 1024
            ),
        )(field.reshape(8, 128, 128), coarse_weight, fine_weight, cotangent.reshape(8, 128, 128))
        output, field_grad, fine, coarse = pl.pallas_call(
            finish,
            out_shape=(
                cells,
                cells,
                jax.ShapeDtypeStruct((27, 16, 256), F32),
                jax.ShapeDtypeStruct((27, 32, 128), F32),
            ),
            in_specs=[inside] * 3,
            out_specs=(inside,) * 4,
        )(output, field_grad, terms)
        return (
            output.reshape(8, 16, 8, 128),
            field_grad.reshape(8, 16, 8, 128),
            fine.transpose(0, 2, 1),
            coarse.transpose(0, 2, 1),
        )

    placed = (P("gx", "gy", "gz", None), P(), P(), P("gx", "gy", "gz", None))
    return jax.shard_map(
        local,
        mesh=mesh,
        in_specs=placed,
        out_specs=(
            P("gx", "gy", "gz", None),
            P("gx", "gy", "gz", None),
            P(None, None, "gz"),
            P(None, None, "gz"),
        ),
        check_vma=False,
    )
```
